256 devices in a mesh: rows: 32 (over y, z), cols: 8 (over x, core).
Axes of the slice: x: 4, y: 4, z: 8, core: 2. Of those that a mesh axis runs over, the one named last changes fastest.
Arguments:
- x_obs: bfloat16 [12288, 256], P(('rows', 'cols')), may hold values from -2 to 2, as said below
- y_gen: bfloat16 [12288, 256], P(('rows', 'cols')), may hold values from -2 to 2.1, as said below
Outputs:
- divergence: float32 [], replicated
- grad_gen: float32 [12288, 256], P(('rows', 'cols'))
The draws below stay inside these ranges and needn't reach their ends.
Inputs may be any that keep to these rules, and one draw needn't show every extreme that they name: `x_obs`: coordinates of observed paths. `y_gen`: coordinates of generated paths.
All inputs are finite; a program needn't handle non-finite values.
Results may differ from the reference program's by a relative error of at most 0.0061.
Values may be sent and summed in bfloat16 or wider, within the bound.
A program may use at most 64 MiB of HBM per device.

```python
import math
import jax
import jax.numpy as jnp
from jax import lax

D = 256
SHARD = 48
ITERS = 3
POINTS = 12288
N_COLS = 8


latent_dims = 8


def latent_spread():
    density = max(POINTS / 16.0, 2.0)
    return math.sqrt(max(density ** (2.0 / latent_dims) - 1.0, 0.25))


def coordinate_gains(key):
    coord_gains = jax.random.uniform(key, (D,), jnp.float32, 0.6, 1.4)
    return coord_gains * math.sqrt(latent_dims / (D * 1.0533))


def draw_x_obs(key, part):
    coord_gains = coordinate_gains(key)
    key = jax.random.fold_in(key, 3)
    key_one, key_two = jax.random.split(key, 2)
    spread_scale = latent_spread()
    noise_scale = 1.3 / math.sqrt(D)
    latents = spread_scale * jax.random.normal(key_one, (POINTS, latent_dims), jnp.float32)
    jitter = noise_scale * jax.random.normal(key_two, (POINTS, D), jnp.float32)
    values = jnp.tile(latents, (1, D // latent_dims)) * coord_gains[None, :] + jitter
    return jnp.clip(values, -2.0, 2.0).astype(jnp.bfloat16)


def draw_y_gen(key, part):
    coord_gains = coordinate_gains(key)
    key = jax.random.fold_in(key, 7)
    key_one, key_two = jax.random.split(key)
    spread_scale = 1.15 * latent_spread()
    latent_shift = 0.3 * latent_spread()
    noise_scale = 1.3 / math.sqrt(D)
    latents = latent_shift + spread_scale * jax.random.normal(key_one, (POINTS, latent_dims), jnp.float32)
    jitter = noise_scale * jax.random.normal(key_two, (POINTS, D), jnp.float32)
    values = jnp.tile(latents, (1, D // latent_dims)) * coord_gains[None, :] + jitter + 0.05
    return jnp.clip(values, -2.0, 2.1).astype(jnp.bfloat16)


def setup_inputs(seed: int = 0) -> dict:
    keys = jax.random.split(jax.random.key(seed), 3)
    return {
        "x_obs": draw_x_obs(jax.random.fold_in(keys[2], 71), 0),
        "y_gen": draw_y_gen(jax.random.fold_in(keys[2], 71), 0),
    }


epsilon = 1.0


def pair_costs(left, right):
    left_f = left.astype(jnp.float32)
    right_f = right.astype(jnp.float32)
    cross = jnp.dot(left_f, right_f.T, precision=lax.Precision.HIGHEST)
    return 0.5 * jnp.sum(left_f * left_f, 1)[:, None] + 0.5 * jnp.sum(right_f * right_f, 1)[None, :] - cross


def in_blocks(array):
    height = SHARD * N_COLS
    return array.reshape((array.shape[0] // height, height) + array.shape[1:])


def row_transform(left, right, potential, log_weight):
    def one_block(block):
        cost = pair_costs(block, right)
        return jax.nn.logsumexp((potential[None, :] - cost) / epsilon, axis=1)

    return -epsilon * (lax.map(one_block, in_blocks(left)).reshape(-1) + log_weight)


def symmetric(points, log_weight, count):
    potential = jnp.zeros((count,), jnp.float32)
    for step in range(ITERS):
        update = row_transform(points, points, potential, log_weight)
        potential = 0.5 * (potential + update)
    return potential


def reference(x_obs, y_gen):
    count = x_obs.shape[0]
    log_weight = -jnp.log(jnp.float32(count))
    left_xy = jnp.zeros((count,), jnp.float32)
    right_xy = jnp.zeros((count,), jnp.float32)
    for step in range(ITERS):
        left_xy = row_transform(x_obs, y_gen, right_xy, log_weight)
        right_xy = row_transform(y_gen, x_obs, left_xy, log_weight)
    self_xx = symmetric(x_obs, log_weight, count)
    self_yy = symmetric(y_gen, log_weight, count)

    def gradient_block(pieces):
        y_block, cross_block, self_block = pieces
        y_float = y_block.astype(jnp.float32)
        cost = pair_costs(y_block, x_obs)
        plan_xy = jnp.exp((cross_block[:, None] + left_xy[None, :] - cost) / epsilon) / count
        cost = pair_costs(y_block, y_gen)
        plan_yy = jnp.exp((self_block[:, None] + self_yy[None, :] - cost) / epsilon) / count
        weight_diff = jnp.sum(plan_xy, 1) - jnp.sum(plan_yy, 1)
        moved = jnp.dot(plan_xy.astype(jnp.bfloat16), x_obs, preferred_element_type=jnp.float32)
        moved = moved - jnp.dot(plan_yy.astype(jnp.bfloat16), y_gen, preferred_element_type=jnp.float32)
        return y_float * weight_diff[:, None] - moved

    grad_gen = lax.map(gradient_block, (in_blocks(y_gen), in_blocks(right_xy), in_blocks(self_yy))).reshape(count, -1)
    divergence = jnp.mean(left_xy - self_xx) + jnp.mean(right_xy - self_yy)
    return divergence, grad_gen
```

```python
import functools
import math

import jax
import jax.numpy as jnp
from jax import lax
from jax.experimental import pallas as pl
from jax.experimental.pallas import tpu as pltpu
from jax.sharding import PartitionSpec as P

MESH = pl.DeviceIdType.MESH
LOG2E = math.log2(math.e)
LANES = 128
XY = 4
Z = 8
GROUP = 16

E_XY = (0, 1, 2, 3, 4, 5)
E_YR = (6, 7, 8)
E_YC = (9, 10, 11)
E_XR = (12, 13, 14)
E_XC = (15, 16)
E_SUM = 17
N_EX = 18


def log2(value):
    return jnp.log(value) * LOG2E


def kernel(
    x_ref, y_ref, div_ref, grad_ref,
    xr, xc, yr, yc,
    a_col, a_row, y_col, y_row, x_col, x_row,
    b_f, b_g, b_qr, b_qc, b_pr, b_pc,
    dense, msg, got, low, weights, own_w, o_send, o_got,
    local_sem, bulk_send, bulk_recv, line_recv, ex_send, ex_recv,
):
    shard = x_ref.shape[0]
    block = xr.shape[0]
    tiles = block // LANES
    points = block * GROUP
    log_n = math.log2(points)

    row, col = lax.axis_index("rows"), lax.axis_index("cols")
    px, core = col // 2, col % 2
    py, pz = row // Z, row % Z
    plane_me = px * XY + py
    line_me = pz * 2 + core

    def at(dx, dy, dz, dc):
        x, y, z, c = (px + dx) % XY, (py + dy) % XY, (pz + dz) % Z, (core + dc) % 2
        return (y * Z + z, x * 2 + c)

    plane = [
        (dx, dy, 0, 0)
        for dx, dy in (
            (2, 2), (1, 2), (3, 2), (2, 1), (2, 3), (1, 1), (3, 3), (1, 3), (3, 1),
            (2, 0), (0, 2), (1, 0), (0, 1), (3, 0), (0, 3),
        )
    ]
    hops = (4, 3, 5, 2, 6, 1, 7)
    line = [(0, 0, dz, dc) for dz in hops for dc in (1, 0)] + [(0, 0, 0, 1)]
    plane_at = [at(*p) for p in plane]
    line_at = [at(*p) for p in line]
    line_same = [at(0, 0, dz, 0) for dz in hops]
    sibling = at(0, 0, 0, 1)

    def slot(ref, index):
        return ref.at[pl.ds(pl.multiple_of(index * shard, 16), shard)]

    own = []
    for n, (src, ref, index) in enumerate(
        ((y_ref, yc, plane_me), (x_ref, xr, line_me), (x_ref, xc, plane_me), (y_ref, yr, line_me))
    ):
        copy = pltpu.make_async_copy(src, slot(ref, index), local_sem.at[n])
        copy.start()
        own.append(copy)

    barrier = pltpu.get_barrier_semaphore()
    for peer in plane_at + line_at:
        pl.semaphore_signal(barrier, inc=1, device_id=peer, device_id_type=MESH)
    msg[...] = jnp.zeros_like(msg)
    for copy in own:
        copy.wait()
    pl.semaphore_wait(barrier, len(plane_at) + len(line_at))

    def send_to(src, dst, send, recv, peer):
        copy = pltpu.make_async_remote_copy(
            src_ref=src, dst_ref=dst, send_sem=send, recv_sem=recv, device_id=peer, device_id_type=MESH
        )
        copy.start()
        return copy

    def wait_bytes(ref, sem):
        pltpu.make_async_copy(ref, ref, sem).wait()

    def gather(which, column, rowwise):
        for n in range(len(plane_at)):
            send_to(
                slot(column, plane_me), slot(column, plane_me), bulk_send.at[which], bulk_recv.at[which], plane_at[n]
            )
            if n < len(hops):
                send_to(
                    slot(rowwise, line_me), slot(rowwise, line_me),
                    bulk_send.at[2 + which], line_recv.at[which, n], line_same[n],
                )
        send_to(
            slot(rowwise, line_me), slot(rowwise, line_me), bulk_send.at[2 + which], bulk_recv.at[2 + which], sibling
        )

    def gather_forward(which, rowwise):
        for n in sorted(range(len(hops)), key=lambda n: min(hops[n], Z - hops[n])):
            source = ((pz + Z - hops[n]) % Z) * 2 + core
            part = slot(rowwise, source)
            wait_bytes(part, line_recv.at[which, n])
            send_to(part, part, bulk_send.at[2 + which], bulk_recv.at[2 + which], sibling)

    def gather_wait(which, column, rowwise):
        wait_bytes(column.at[pl.ds(0, 15 * shard)], bulk_recv.at[which])
        wait_bytes(rowwise.at[pl.ds(0, 8 * shard)], bulk_recv.at[2 + which])

    def send(ex, along_line):
        peers, me = (line_at, line_me) if along_line else (plane_at, plane_me)
        for peer in peers:
            send_to(msg.at[ex], got.at[ex, me], ex_send.at[ex], ex_recv.at[ex], peer)
        got[ex, me] = msg[ex]

    def receive(ex):
        wait_bytes(got.at[ex, pl.ds(0, GROUP - 1)], ex_recv.at[ex])

    def combined(ex):
        parts = got[ex]
        peak = jnp.max(parts, 0)
        return peak + log2(jnp.sum(jnp.exp2(parts - peak[None]), 0))

    def spread(index, out):
        def step(k, carry):
            out[pl.ds(pl.multiple_of(k * LANES, LANES), LANES), :] = jnp.broadcast_to(
                dense[index, pl.ds(k, 1), :], (LANES, LANES)
            ).T
            return carry

        lax.fori_loop(0, tiles, step, 0)

    def compact(src, store):
        def step(k, carry):
            store(k, src[pl.ds(pl.multiple_of(k * LANES, LANES), LANES), :].T[0:1, :])
            return carry

        lax.fori_loop(0, tiles, step, 0)

    def half_norms(block_ref, out):
        def step(k, carry):
            rows = pl.ds(pl.multiple_of(k * LANES, LANES), LANES)
            v = block_ref[rows, :].astype(jnp.float32)
            out[rows, :] = jnp.broadcast_to(
                (-0.5 * LOG2E) * jnp.sum(v * v, 1, keepdims=True), (LANES, LANES)
            )
            return carry

        lax.fori_loop(0, tiles, step, 0)

    def products(left, right, out):
        def pair(k, carry):
            both = LOG2E * lax.dot_general(
                left[...],
                right[pl.ds(pl.multiple_of(k * LANES * 2, LANES * 2), LANES * 2), :],
                (((1,), (1,)), ((), ())),
                preferred_element_type=jnp.float32,
            )
            out[2 * k] = both[:, :LANES]
            out[2 * k + 1] = both[:, LANES:]
            return carry

        lax.fori_loop(0, tiles // 2, pair, 0)

    def partial_lse(scores, potential, ex):
        part = 192

        def step(k, carry):
            peak = total = None
            for n in range(block // part):
                rows = pl.ds(n * part, part)
                s = (scores[k, rows, :] + potential[rows, :]).reshape(part // 8, 8, LANES)
                peak_n = jnp.max(s, 0)
                total_n = jnp.sum(jnp.exp2(s - peak_n[None]), 0)
                if peak is None:
                    peak, total = peak_n, total_n
                else:
                    both = jnp.maximum(peak, peak_n)
                    total = total * jnp.exp2(peak - both) + total_n * jnp.exp2(peak_n - both)
                    peak = both
            top = jnp.max(peak, 0, keepdims=True)
            msg[ex, pl.ds(k, 1), :] = top + log2(jnp.sum(total * jnp.exp2(peak - top), 0, keepdims=True))
            return carry

        lax.fori_loop(0, tiles, step, 0)

    D_F, D_G, D_QR, D_QC, D_PR, D_PC = range(6)

    def cross_update(ex, index, out):
        receive(ex)
        dense[index] = log_n - combined(ex)
        if out is not None:
            spread(index, out)

    def self_update(ex, index, out):
        receive(ex)
        dense[index] = 0.5 * (dense[index] + log_n - combined(ex))
        if out is not None:
            spread(index, out)

    def start_dense(index, src):
        def store(k, value):
            dense[index, pl.ds(k, 1), :] = value

        compact(src, store)

    dense[...] = jnp.zeros_like(dense)

    gather(0, yc, xr)
    gather_forward(0, xr)
    gather_wait(0, yc, xr)
    half_norms(yc, b_g)
    products(yc, xr, a_row)
    partial_lse(a_row, b_g, E_XY[0])
    send(E_XY[0], True)
    gather(1, xc, yr)
    products(xr, yc, a_col)
    b_qc[...] = b_g[...]
    start_dense(D_QC, b_qc)
    half_norms(xr, b_pr)
    start_dense(D_PR, b_pr)

    cross_update(E_XY[0], D_F, b_f)
    partial_lse(a_col, b_f, E_XY[1])
    send(E_XY[1], False)

    gather_forward(1, yr)
    gather_wait(1, xc, yr)
    half_norms(yr, b_qr)
    start_dense(D_QR, b_qr)
    products(yc, yr, y_row)
    products(yr, yc, y_col)
    partial_lse(y_row, b_qc, E_YR[0])
    send(E_YR[0], True)
    partial_lse(y_col, b_qr, E_YC[0])
    send(E_YC[0], False)

    cross_update(E_XY[1], D_G, b_g)
    partial_lse(a_row, b_g, E_XY[2])
    send(E_XY[2], True)

    half_norms(xc, b_pc)
    start_dense(D_PC, b_pc)
    products(xc, xr, x_row)
    products(xr, xc, x_col)
    partial_lse(x_row, b_pc, E_XR[0])
    send(E_XR[0], True)
    partial_lse(x_col, b_pr, E_XC[0])
    send(E_XC[0], False)

    cross_update(E_XY[2], D_F, b_f)
    partial_lse(a_col, b_f, E_XY[3])
    send(E_XY[3], False)

    self_update(E_YR[0], D_QR, b_qr)
    self_update(E_YC[0], D_QC, b_qc)
    partial_lse(y_row, b_qc, E_YR[1])
    send(E_YR[1], True)
    partial_lse(y_col, b_qr, E_YC[1])
    send(E_YC[1], False)

    cross_update(E_XY[3], D_G, b_g)
    partial_lse(a_row, b_g, E_XY[4])
    send(E_XY[4], True)

    self_update(E_XR[0], D_PR, b_pr)
    self_update(E_XC[0], D_PC, b_pc)
    partial_lse(x_row, b_pc, E_XR[1])
    send(E_XR[1], True)
    partial_lse(x_col, b_pr, E_XC[1])
    send(E_XC[1], False)
    self_update(E_YR[1], D_QR, b_qr)
    self_update(E_YC[1], D_QC, b_qc)
    partial_lse(y_row, b_qc, E_YR[2])
    send(E_YR[2], True)
    partial_lse(y_col, b_qr, E_YC[2])
    send(E_YC[2], False)

    cross_update(E_XY[4], D_F, None)

    group = 32

    def last_step(n, carry):
        rows = pl.ds(pl.multiple_of(n * group, group), group)
        scores = [a_row[k, rows, :] + dense[D_F, k : k + 1, :] for k in range(tiles)]
        peak = jnp.max(functools.reduce(jnp.maximum, scores), 1, keepdims=True)
        parts = [jnp.exp2(s - peak) for s in scores]
        rounded = [p.astype(jnp.bfloat16) for p in parts]
        total = jnp.sum(functools.reduce(jnp.add, parts), 1, keepdims=True)
        total_low = jnp.sum(functools.reduce(jnp.add, [r.astype(jnp.float32) for r in rounded]), 1, keepdims=True)
        for k in range(tiles):
            low[rows, pl.ds(k * LANES, LANES)] = rounded[k]
        b_f[rows, :] = jnp.broadcast_to(peak + log2(total), (group, LANES))
        b_pc[rows, :] = jnp.broadcast_to(1.0 / total, (group, LANES))
        b_pr[rows, :] = jnp.broadcast_to(total_low, (group, LANES))
        return carry

    lax.fori_loop(0, block // group, last_step, 0)

    def moved(index, scaled, blocks):
        def step(n, carry):
            rows = pl.ds(pl.multiple_of(n * LANES, LANES), LANES)
            product = jnp.dot(low[rows, :], blocks[...], preferred_element_type=jnp.float32)
            for k in range(2):
                lanes = pl.ds(k * LANES, LANES)
                value = product[:, k * LANES : (k + 1) * LANES] - b_pr[rows, :] * yc[rows, lanes].astype(jnp.float32)
                if scaled:
                    value = value * b_pc[rows, :]
                o_send[index, rows, lanes] = value.astype(jnp.bfloat16)
            return carry

        lax.fori_loop(0, block // LANES, step, 0)

    def scatter(index):
        for p, peer in zip(plane, plane_at):
            target = ((px + p[0]) % XY) * XY + (py + p[1]) % XY
            send_to(
                slot(o_send.at[index], target), o_got.at[index, plane_me],
                bulk_send.at[4 + index], bulk_recv.at[4 + index], peer,
            )
        o_got[index, plane_me] = o_send[index, pl.ds(pl.multiple_of(plane_me * shard, 16), shard), :]

    def store_last(k, value):
        msg[E_XY[5], pl.ds(k, 1), :] = value

    compact(b_f, store_last)
    self_update(E_XR[1], D_PR, None)
    self_update(E_XC[1], D_PC, None)
    moved(0, True, xr)
    scatter(0)

    spread(D_PC, b_pc)
    partial_lse(x_row, b_pc, E_XR[2])
    send(E_XR[2], True)
    self_update(E_YR[2], D_QR, b_qr)
    self_update(E_YC[2], D_QC, b_qc)

    def plan_step(n, carry):
        rows = pl.ds(pl.multiple_of(n * group, group), group)
        total = None
        for k in range(tiles):
            plan = jnp.exp2(y_row[k, rows, :] + (dense[D_QR, k : k + 1, :] - log_n) + b_qc[rows, :])
            low[rows, pl.ds(k * LANES, LANES)] = plan.astype(jnp.bfloat16)
            total = plan if total is None else total + plan
        b_pr[rows, :] = jnp.broadcast_to(jnp.sum(total, 1, keepdims=True), (group, LANES))
        return carry

    lax.fori_loop(0, block // group, plan_step, 0)
    moved(1, False, yr)
    scatter(1)
    self_update(E_XR[2], D_PR, None)

    used = lax.broadcasted_iota(jnp.int32, (8, LANES), 0) < tiles
    here = jnp.where(used, dense[D_F] - dense[D_PR] - dense[D_QR], 0.0)
    msg[E_XY[5], pl.ds(tiles, 1), :] = jnp.sum(here, 0, keepdims=True)
    send(E_XY[5], False)

    receive(E_XY[5])
    parts = got[E_XY[5]]
    lse = combined(E_XY[5])
    dense[D_G] = log_n - lse
    weights[...] = jnp.exp2(parts - lse[None])
    msg[E_SUM] = jnp.where(used, dense[D_G], 0.0)
    send(E_SUM, True)
    others = jnp.sum(parts, 0)[tiles : tiles + 1, :]
    for k in range(tiles):
        rows = jnp.concatenate([weights[:, k, :], jnp.zeros((LANES - GROUP, LANES), jnp.float32)], 0)
        own_w[pl.ds(k * LANES, LANES), :] = rows.T
    mine = own_w[pl.ds(pl.multiple_of(plane_me * shard, 16), shard), :]

    wait_bytes(o_got.at[0, pl.ds(0, GROUP - 1)], bulk_recv.at[4])
    wait_bytes(o_got.at[1, pl.ds(0, GROUP - 1)], bulk_recv.at[5])
    grad = jnp.zeros(grad_ref.shape, jnp.float32)
    for n in range(GROUP):
        grad = grad + o_got[1, n].astype(jnp.float32)
        grad = grad - mine[:, n : n + 1] * o_got[0, n].astype(jnp.float32)
    grad_ref[...] = grad

    receive(E_SUM)
    total = jnp.sum(jnp.sum(got[E_SUM], 0), 0, keepdims=True) + others
    div_ref[...] = jnp.broadcast_to(
        jnp.sum(total, 1, keepdims=True) * (1.0 / (LOG2E * points)), div_ref.shape
    )

    for which, (column, rowwise) in enumerate(((yc, xr), (xc, yr))):
        wait_bytes(column.at[pl.ds(0, 15 * shard)], bulk_send.at[which])
        wait_bytes(rowwise.at[pl.ds(0, 15 * shard)], bulk_send.at[2 + which])
    for index in range(2):
        wait_bytes(o_got.at[index, pl.ds(0, GROUP - 1)], bulk_send.at[4 + index])
    for ex in range(N_EX):
        wait_bytes(got.at[ex, pl.ds(0, GROUP - 1)], ex_send.at[ex])


def shards(x_obs, y_gen):
    shard, width = x_obs.shape
    block = shard * GROUP
    tiles = block // LANES
    f32, bf16 = jnp.float32, jnp.bfloat16
    div, grad = pl.pallas_call(
        kernel,
        out_shape=(jax.ShapeDtypeStruct((8, LANES), f32), jax.ShapeDtypeStruct((shard, width), f32)),
        in_specs=[pl.BlockSpec(memory_space=pl.ANY)] * 2,
        out_specs=(pl.BlockSpec(memory_space=pltpu.VMEM), pl.BlockSpec(memory_space=pltpu.VMEM)),
        scratch_shapes=[
            *[pltpu.VMEM((block, width), bf16)] * 4,
            *[pltpu.VMEM((tiles, block, LANES), f32)] * 6,
            *[pltpu.VMEM((block, LANES), f32)] * 6,
            pltpu.VMEM((6, 8, LANES), f32),
            pltpu.VMEM((N_EX, 8, LANES), f32),
            pltpu.VMEM((N_EX, GROUP, 8, LANES), f32),
            pltpu.VMEM((block, block), bf16),
            pltpu.VMEM((GROUP, 8, LANES), f32),
            pltpu.VMEM((block, LANES), f32),
            pltpu.VMEM((2, block, width), bf16),
            pltpu.VMEM((2, GROUP, shard, width), bf16),
            pltpu.SemaphoreType.DMA((4,)),
            pltpu.SemaphoreType.DMA((6,)),
            pltpu.SemaphoreType.DMA((6,)),
            pltpu.SemaphoreType.DMA((2, 7)),
            pltpu.SemaphoreType.DMA((N_EX,)),
            pltpu.SemaphoreType.DMA((N_EX,)),
        ],
        compiler_params=pltpu.CompilerParams(
            collective_id=0, has_side_effects=True, vmem_limit_bytes=48 * 1024 * 1024
        ),
    )(x_obs, y_gen)
    return div[0, 0], grad


def solution(mesh):
    placed = P(("rows", "cols"), None)
    return jax.shard_map(
        shards, mesh=mesh, in_specs=(placed, placed), out_specs=(P(), placed), check_vma=False
    )
```

```python
import math

import jax
import jax.numpy as jnp
from jax import lax
from jax.experimental import pallas as pl
from jax.experimental.pallas import tpu as pltpu
from jax.sharding import PartitionSpec as P

MESH = pl.DeviceIdType.MESH
LOG2E = math.log2(math.e)
LANES = 128
XY = 4
Z = 8
GROUP = 16

E_XY = (0, 1, 2, 3, 4, 5)
E_YR = (6, 7, 8)
E_YC = (9, 10, 11)
E_XR = (12, 13)
E_XC = (14, 15, 16)
E_SUM = 17
N_EX = 18


def log2(value):
    return jnp.log(value) * LOG2E


def kernel(
    x_ref, y_ref, div_ref, grad_ref,
    xr, xc, yr, yc,
    a_col, a_row, y_own, x_own,
    b_f, b_g, b_ny, b_nx, b_vy, b_vx,
    dense, msg, got, weights, own_w, o_send, o_got,
    local_sem, bulk_send, bulk_recv, line_recv, ex_send, ex_recv,
):
    shard = xr.shape[0] // GROUP
    block = xr.shape[0]
    tiles = block // LANES
    points = block * GROUP
    log_n = math.log2(points)

    row, col = lax.axis_index("rows"), lax.axis_index("cols")
    px, core = col // 2, col % 2
    py, pz = row // Z, row % Z
    plane_me = px * XY + py
    line_me = pz * 2 + core

    def at(dx, dy, dz, dc):
        x, y, z, c = (px + dx) % XY, (py + dy) % XY, (pz + dz) % Z, (core + dc) % 2
        return (y * Z + z, x * 2 + c)

    plane = [
        (dx, dy, 0, 0)
        for dx, dy in (
            (2, 2), (1, 2), (3, 2), (2, 1), (2, 3), (1, 1), (3, 3), (1, 3), (3, 1),
            (2, 0), (0, 2), (1, 0), (0, 1), (3, 0), (0, 3),
        )
    ]
    hops = (4, 3, 5, 2, 6, 1, 7)
    line = [(0, 0, dz, dc) for dz in hops for dc in (1, 0)] + [(0, 0, 0, 1)]
    plane_at = [at(*p) for p in plane]
    line_at = [at(*p) for p in line]
    line_same = [at(0, 0, dz, 0) for dz in hops]
    sibling = at(0, 0, 0, 1)

    def slot(ref, index):
        return ref.at[pl.ds(pl.multiple_of(index * shard, 16), shard)]

    barrier = pltpu.get_barrier_semaphore()
    for peer in line_at + plane_at:
        pl.semaphore_signal(barrier, inc=1, device_id=peer, device_id_type=MESH)

    own = []
    for n, (src, ref, index) in enumerate(
        ((y_ref, yc, plane_me), (x_ref, xr, line_me), (x_ref, xc, plane_me), (y_ref, yr, line_me))
    ):
        copy = pltpu.make_async_copy(src, slot(ref, index), local_sem.at[n])
        copy.start()
        own.append(copy)
    msg[...] = jnp.ones_like(msg)
    dense[...] = jnp.ones_like(dense)
    b_vy[...] = jnp.ones_like(b_vy)
    b_vx[...] = jnp.ones_like(b_vx)
    for copy in own:
        copy.wait()
    pl.semaphore_wait(barrier, len(plane_at) + len(line_at))

    def send_to(src, dst, send, recv, peer):
        copy = pltpu.make_async_remote_copy(
            src_ref=src, dst_ref=dst, send_sem=send, recv_sem=recv, device_id=peer, device_id_type=MESH
        )
        copy.start()
        return copy

    def wait_bytes(ref, sem):
        pltpu.make_async_copy(ref, ref, sem).wait()

    def send_plane(which, column, n):
        send_to(slot(column, plane_me), slot(column, plane_me), bulk_send.at[which], bulk_recv.at[which], plane_at[n])

    def send_line(which, rowwise, n):
        part = slot(rowwise, line_me)
        if n < len(hops):
            send_to(part, part, bulk_send.at[2 + which], line_recv.at[which, n], line_same[n])
        else:
            send_to(part, part, bulk_send.at[2 + which], bulk_recv.at[2 + which], sibling)

    def gather(which, column, rowwise):
        for n in range(len(plane_at)):
            if rowwise is not None and n <= len(hops):
                send_line(which, rowwise, n)
            if column is not None:
                send_plane(which, column, n)

    def gather_forward(which, rowwise):
        for n in sorted(range(len(hops)), key=lambda n: min(hops[n], Z - hops[n])):
            source = ((pz + Z - hops[n]) % Z) * 2 + core
            part = slot(rowwise, source)
            wait_bytes(part, line_recv.at[which, n])
            send_to(part, part, bulk_send.at[2 + which], bulk_recv.at[2 + which], sibling)

    def gather_plane(which, column):
        wait_bytes(column.at[pl.ds(0, 15 * shard)], bulk_recv.at[which])

    def gather_line(which, rowwise):
        wait_bytes(rowwise.at[pl.ds(0, 8 * shard)], bulk_recv.at[2 + which])

    def send(ex, along_line):
        peers, me = (line_at, line_me) if along_line else (plane_at, plane_me)
        for peer in peers:
            send_to(msg.at[ex], got.at[ex, me], ex_send.at[ex], ex_recv.at[ex], peer)
        got[ex, me] = msg[ex]

    def receive(ex):
        wait_bytes(got.at[ex, pl.ds(0, GROUP - 1)], ex_recv.at[ex])

    def combined(ex):
        parts = got[ex]
        peak = jnp.max(parts, 0)
        return peak + log2(jnp.sum(jnp.exp2(parts - peak[None]), 0))

    def spread(index, out):
        for k in range(tiles):
            out[k * LANES : (k + 1) * LANES, :] = jnp.broadcast_to(dense[index, k : k + 1, :], (LANES, LANES)).T

    def half_norms(block_ref, out, index):
        v = block_ref[...].astype(jnp.float32)
        v = v * v
        high = v.astype(jnp.bfloat16)
        rest = (v - high.astype(jnp.float32)).astype(jnp.bfloat16)
        if out is not None:
            ones = jnp.full((v.shape[1], LANES), 1.0, jnp.bfloat16)
            out[...] = (-0.5 * LOG2E) * (
                jnp.dot(high, ones, preferred_element_type=jnp.float32)
                + jnp.dot(rest, ones, preferred_element_type=jnp.float32)
            )
        if index is not None:
            ones = jnp.full((8, v.shape[1]), 1.0, jnp.bfloat16)
            dims = (((1,), (1,)), ((), ()))
            value = (-0.5 * LOG2E) * (
                lax.dot_general(ones, high, dims, preferred_element_type=jnp.float32)
                + lax.dot_general(ones, rest, dims, preferred_element_type=jnp.float32)
            )
            for k in range(tiles):
                dense[index, k : k + 1, :] = value[0:1, k * LANES : (k + 1) * LANES]

    def products(left, right, out, norm_left=None, norm_right=None):
        wide = 2 * LANES
        for k in range(0, tiles, 2):
            both = LOG2E * lax.dot_general(
                left[...],
                right[k * LANES : k * LANES + wide, :],
                (((1,), (1,)), ((), ())),
                preferred_element_type=jnp.float32,
            )
            for h in range(2):
                part = both[:, h * LANES : (h + 1) * LANES]
                if norm_left is not None:
                    part = jnp.exp2(part + norm_left[...] + dense[norm_right, k + h : k + h + 1, :])
                out[k + h] = part

    def partial_lse(scores, potential, ex):
        part, together = 64, 3

        def step(first, carry):
            state = [None] * together
            for n in range(block // part):
                rows = pl.ds(n * part, part)
                p = potential[rows, :]
                for u in range(together):
                    s = (scores[first * together + u, rows, :] + p).reshape(part // 8, 8, LANES)
                    peak = jnp.max(s, 0)
                    total = jnp.sum(jnp.exp2(s - peak[None]), 0)
                    if n:
                        both = jnp.maximum(state[u][0], peak)
                        total = state[u][1] * jnp.exp2(state[u][0] - both) + total * jnp.exp2(peak - both)
                        peak = both
                    state[u] = (peak, total)
            for u, (peak, total) in enumerate(state):
                top = jnp.max(peak, 0, keepdims=True)
                msg[ex, pl.ds(first * together + u, 1), :] = top + log2(
                    jnp.sum(total * jnp.exp2(peak - top), 0, keepdims=True)
                )
            return carry

        lax.fori_loop(0, tiles // together, step, 0)

    def self_sums(kernel_ref, v_column, v_row, ex_row, ex_col):
        part, together = 32, 3

        def step(first, carry):
            down = list(carry)
            for u in range(together):
                n = first * together + u
                across = []
                for g in range(LANES // part):
                    rows = pl.ds(pl.multiple_of(n * LANES + g * part, part), part)
                    total = None
                    for k in range(tiles):
                        tile = kernel_ref[k, rows, :]
                        if ex_row is not None:
                            down[k] = down[k] + jnp.sum((tile * v_column[rows, :]).reshape(part // 8, 8, LANES), 0)
                        term = tile * dense[v_row, k : k + 1, :]
                        total = term if total is None else total + term
                    across.append(total)
                msg[ex_col, pl.ds(n, 1), :] = jnp.sum(jnp.concatenate(across, 0).T, 0, keepdims=True)
            return tuple(down)

        first = tuple(jnp.zeros((8, LANES), jnp.float32) for _ in range(tiles if ex_row is not None else 0))
        down = lax.fori_loop(0, tiles // together, step, first)
        for k, value in enumerate(down):
            msg[ex_row, k : k + 1, :] = jnp.sum(value, 0, keepdims=True)

    D_F, D_G, D_NX, D_NY, D_VXR, D_VXC, D_VYR, D_VYC = range(8)

    def cross_update(ex, index, out):
        receive(ex)
        dense[index] = log_n - combined(ex)
        if out is not None:
            spread(index, out)

    def self_update(ex, index, out):
        receive(ex)
        dense[index] = jnp.sqrt(dense[index] * points / jnp.sum(got[ex], 0))
        if out is not None:
            spread(index, out)

    def moved(index, weight, rows_ref):
        quarter = shard * XY
        ones = jnp.full((block, LANES), 1.0, jnp.bfloat16)
        for dx in (2, 1, 3, 0):
            qx = (px + dx) % XY
            rows = pl.ds(pl.multiple_of(qx * quarter, 16), quarter)
            low = jnp.concatenate([weight(k, rows).astype(jnp.bfloat16) for k in range(tiles)], 1)
            product = jnp.dot(low, rows_ref[...], preferred_element_type=jnp.float32)
            total = jnp.dot(low, ones, preferred_element_type=jnp.float32)
            for k in range(2):
                lanes = pl.ds(k * LANES, LANES)
                value = product[:, k * LANES : (k + 1) * LANES] - total * yc[rows, lanes].astype(jnp.float32)
                o_send[index, rows, lanes] = value.astype(jnp.bfloat16)
            for dy in (2, 1, 3, 0):
                if dx or dy:
                    send_to(
                        slot(o_send.at[index], qx * XY + (py + dy) % XY), o_got.at[index, plane_me],
                        bulk_send.at[4 + index], bulk_recv.at[4 + index], at(dx, dy, 0, 0),
                    )
        o_got[index, plane_me] = o_send[index, pl.ds(pl.multiple_of(plane_me * shard, 16), shard), :]

    def plan_yy(k, rows):
        return y_own[k, rows, :] * (dense[D_VYR, k : k + 1, :] * (1.0 / points)) * b_vy[rows, :]

    def plan_xy(k, rows):
        return jnp.exp2(a_row[k, rows, :] + dense[D_F, k : k + 1, :] - b_g[rows, :])

    gather(0, yc, xr)
    gather(1, None, yr)
    gather_forward(0, xr)
    gather_plane(0, yc)
    half_norms(yc, b_ny, None)
    gather_line(0, xr)
    products(yc, xr, a_row)
    partial_lse(a_row, b_ny, E_XY[0])
    send(E_XY[0], True)

    gather(1, xc, None)
    products(xr, yc, a_col)
    half_norms(xr, None, D_NX)
    gather_forward(1, yr)
    gather_line(1, yr)
    half_norms(yr, None, D_NY)
    products(yc, yr, y_own, b_ny, D_NY)
    self_sums(y_own, b_vy, D_VYR, E_YR[0], E_YC[0])
    send(E_YR[0], True)
    send(E_YC[0], False)

    cross_update(E_XY[0], D_F, b_f)
    partial_lse(a_col, b_f, E_XY[1])
    send(E_XY[1], False)

    gather_plane(1, xc)
    half_norms(xc, b_nx, None)
    products(xc, xr, x_own, b_nx, D_NX)
    self_sums(x_own, b_vx, D_VXR, E_XR[0], E_XC[0])
    send(E_XR[0], True)
    send(E_XC[0], False)

    cross_update(E_XY[1], D_G, b_g)
    partial_lse(a_row, b_g, E_XY[2])
    send(E_XY[2], True)

    self_update(E_YR[0], D_VYR, None)
    self_update(E_YC[0], D_VYC, b_vy)
    self_sums(y_own, b_vy, D_VYR, E_YR[1], E_YC[1])
    send(E_YR[1], True)
    send(E_YC[1], False)

    cross_update(E_XY[2], D_F, b_f)
    partial_lse(a_col, b_f, E_XY[3])
    send(E_XY[3], False)

    self_update(E_YR[1], D_VYR, None)
    self_update(E_YC[1], D_VYC, b_vy)
    self_sums(y_own, b_vy, D_VYR, E_YR[2], E_YC[2])
    send(E_YR[2], True)
    send(E_YC[2], False)
    self_update(E_XR[0], D_VXR, None)
    self_update(E_XC[0], D_VXC, b_vx)
    self_sums(x_own, b_vx, D_VXR, E_XR[1], E_XC[1])
    send(E_XR[1], True)
    send(E_XC[1], False)

    cross_update(E_XY[3], D_G, b_g)
    partial_lse(a_row, b_g, E_XY[4])
    send(E_XY[4], True)

    self_update(E_YR[2], D_VYR, None)
    self_update(E_YC[2], D_VYC, b_vy)
    moved(1, plan_yy, yr)
    self_update(E_XR[1], D_VXR, None)
    self_update(E_XC[1], D_VXC, None)
    self_sums(x_own, None, D_VXR, None, E_XC[2])
    send(E_XC[2], False)

    cross_update(E_XY[4], D_F, b_f)
    partial_lse(a_col, b_f, E_XY[5])
    dense[D_G] = msg[E_XY[5]]
    used = lax.broadcasted_iota(jnp.int32, (8, LANES), 0) < tiles
    here = jnp.where(used, dense[D_F] - dense[D_NX] - dense[D_NY] - log2(dense[D_VYR]), 0.0)
    msg[E_XY[5], tiles : tiles + 1, :] = jnp.sum(here, 0, keepdims=True)
    send(E_XY[5], False)
    spread(D_G, b_g)
    moved(0, plan_xy, xr)
    self_update(E_XC[2], D_VXC, None)

    receive(E_XY[5])
    parts = got[E_XY[5]]
    lse = combined(E_XY[5])
    msg[E_SUM] = jnp.where(used, log_n - lse - log2(dense[D_VXC]), 0.0)
    send(E_SUM, True)
    weights[...] = jnp.exp2(parts - lse[None])
    others = jnp.sum(parts, 0)[tiles : tiles + 1, :]
    for k in range(tiles):
        rows = jnp.concatenate([weights[:, k, :], jnp.zeros((LANES - GROUP, LANES), jnp.float32)], 0)
        own_w[pl.ds(k * LANES, LANES), :] = rows.T
    mine = own_w[pl.ds(pl.multiple_of(plane_me * shard, 16), shard), :]

    wait_bytes(o_got.at[1, pl.ds(0, GROUP - 1)], bulk_recv.at[5])
    grad = jnp.sum(o_got[1].astype(jnp.float32), 0)
    wait_bytes(o_got.at[0, pl.ds(0, GROUP - 1)], bulk_recv.at[4])
    for n in range(GROUP):
        grad = grad - mine[:, n : n + 1] * o_got[0, n].astype(jnp.float32)
    grad_ref[...] = grad

    receive(E_SUM)
    total = jnp.sum(jnp.sum(got[E_SUM], 0), 0, keepdims=True) + others
    div_ref[...] = jnp.broadcast_to(
        jnp.sum(total, 1, keepdims=True) * (1.0 / (LOG2E * points)), div_ref.shape
    )

    for which, (column, rowwise) in enumerate(((yc, xr), (xc, yr))):
        wait_bytes(column.at[pl.ds(0, 15 * shard)], bulk_send.at[which])
        wait_bytes(rowwise.at[pl.ds(0, 15 * shard)], bulk_send.at[2 + which])
    for index in range(2):
        wait_bytes(o_got.at[index, pl.ds(0, GROUP - 1)], bulk_send.at[4 + index])
    for ex in range(N_EX):
        wait_bytes(got.at[ex, pl.ds(0, GROUP - 1)], ex_send.at[ex])


def shards(x_obs, y_gen):
    shard, width = x_obs.shape
    block = shard * GROUP
    tiles = block // LANES
    f32, bf16 = jnp.float32, jnp.bfloat16
    div, grad = pl.pallas_call(
        kernel,
        out_shape=(jax.ShapeDtypeStruct((8, LANES), f32), jax.ShapeDtypeStruct((shard, width), f32)),
        in_specs=[pl.BlockSpec(memory_space=pltpu.HBM)] * 2,
        out_specs=(pl.BlockSpec(memory_space=pltpu.VMEM), pl.BlockSpec(memory_space=pltpu.VMEM)),
        scratch_shapes=[
            *[pltpu.VMEM((block, width), bf16)] * 4,
            *[pltpu.VMEM((tiles, block, LANES), f32)] * 4,
            *[pltpu.VMEM((block, LANES), f32)] * 6,
            pltpu.VMEM((8, 8, LANES), f32),
            pltpu.VMEM((N_EX, 8, LANES), f32),
            pltpu.VMEM((N_EX, GROUP, 8, LANES), f32),
            pltpu.VMEM((GROUP, 8, LANES), f32),
            pltpu.VMEM((block, LANES), f32),
            pltpu.VMEM((2, block, width), bf16),
            pltpu.VMEM((2, GROUP, shard, width), bf16),
            pltpu.SemaphoreType.DMA((4,)),
            pltpu.SemaphoreType.DMA((6,)),
            pltpu.SemaphoreType.DMA((6,)),
            pltpu.SemaphoreType.DMA((2, 7)),
            pltpu.SemaphoreType.DMA((N_EX,)),
            pltpu.SemaphoreType.DMA((N_EX,)),
        ],
        compiler_params=pltpu.CompilerParams(
            collective_id=0, has_side_effects=True, vmem_limit_bytes=48 * 1024 * 1024
        ),
    )(x_obs, y_gen)
    return div[0, 0], grad


def solution(mesh):
    placed = P(("rows", "cols"), None)
    return jax.shard_map(
        shards, mesh=mesh, in_specs=(placed, placed), out_specs=(P(), placed), check_vma=False
    )
```

```python
import math

import jax
import jax.numpy as jnp
from jax import lax
from jax.experimental import pallas as pl
from jax.experimental.pallas import tpu as pltpu
from jax.sharding import PartitionSpec as P

MESH = pl.DeviceIdType.MESH
LOG2E = math.log2(math.e)
LANES = 128
XY = 4
Z = 8
GROUP = 16

E_XY = (0, 1, 2, 3, 4, 5)
E_YR = (6, 7, 8)
E_YC = (9, 10)
E_XR = (11, 12)
E_XC = (13, 14, 15)
E_SUM = 16
N_EX = 17


def log2(value):
    return jnp.log(value) * LOG2E


def kernel(
    x_ref, y_ref, div_ref, grad_ref,
    xr, xc, yr, yc,
    a_col, a_row, y_own, x_own,
    b_f, b_g, b_ny, b_nx, b_vy, b_vx,
    dense, msg, got, sum_msg, sum_got, o_send, o_got,
    local_sem, bulk_send, bulk_recv, line_recv, ex_send, ex_recv,
):
    shard = xr.shape[0] // GROUP
    block = xr.shape[0]
    tiles = block // LANES
    points = block * GROUP
    log_n = math.log2(points)

    row, col = lax.axis_index("rows"), lax.axis_index("cols")
    px, core = col // 2, col % 2
    py, pz = row // Z, row % Z
    plane_me = px * XY + py
    line_me = pz * 2 + core

    def at(dx, dy, dz, dc):
        x, y, z, c = (px + dx) % XY, (py + dy) % XY, (pz + dz) % Z, (core + dc) % 2
        return (y * Z + z, x * 2 + c)

    plane = [
        (dx, dy, 0, 0)
        for dx, dy in (
            (2, 2), (1, 2), (3, 2), (2, 1), (2, 3), (1, 1), (3, 3), (1, 3), (3, 1),
            (2, 0), (0, 2), (1, 0), (0, 1), (3, 0), (0, 3),
        )
    ]
    hops = (4, 3, 5, 2, 6, 1, 7)
    line = [(0, 0, dz, dc) for dz in hops for dc in (1, 0)] + [(0, 0, 0, 1)]
    plane_at = [at(*p) for p in plane]
    line_at = [at(*p) for p in line]
    line_same = [at(0, 0, dz, 0) for dz in hops]
    sibling = at(0, 0, 0, 1)

    def slot(ref, index):
        return ref.at[pl.ds(pl.multiple_of(index * shard, 16), shard)]

    barrier = pltpu.get_barrier_semaphore()
    for peer in line_at + plane_at:
        pl.semaphore_signal(barrier, inc=1, device_id=peer, device_id_type=MESH)

    own = []
    for n, (src, ref, index) in enumerate(
        ((y_ref, yc, plane_me), (x_ref, xr, line_me), (x_ref, xc, plane_me), (y_ref, yr, line_me))
    ):
        copy = pltpu.make_async_copy(src, slot(ref, index), local_sem.at[n])
        copy.start()
        own.append(copy)
    msg[...] = jnp.ones_like(msg)
    dense[...] = jnp.ones_like(dense)
    b_vy[...] = jnp.ones_like(b_vy)
    b_vx[...] = jnp.ones_like(b_vx)
    for copy in own:
        copy.wait()
    pl.semaphore_wait(barrier, len(plane_at) + len(line_at))

    def send_to(src, dst, send, recv, peer):
        copy = pltpu.make_async_remote_copy(
            src_ref=src, dst_ref=dst, send_sem=send, recv_sem=recv, device_id=peer, device_id_type=MESH
        )
        copy.start()
        return copy

    def wait_bytes(ref, sem):
        pltpu.make_async_copy(ref, ref, sem).wait()

    def send_plane(which, column, n):
        send_to(slot(column, plane_me), slot(column, plane_me), bulk_send.at[which], bulk_recv.at[which], plane_at[n])

    def send_line(which, rowwise, n):
        part = slot(rowwise, line_me)
        if n < len(hops):
            send_to(part, part, bulk_send.at[2 + which], line_recv.at[which, n], line_same[n])
        else:
            send_to(part, part, bulk_send.at[2 + which], bulk_recv.at[2 + which], sibling)

    def gather(which, column, rowwise):
        for n in range(len(plane_at)):
            if rowwise is not None and n <= len(hops):
                send_line(which, rowwise, n)
            if column is not None:
                send_plane(which, column, n)

    def gather_forward(which, rowwise):
        for n in sorted(range(len(hops)), key=lambda n: min(hops[n], Z - hops[n])):
            source = ((pz + Z - hops[n]) % Z) * 2 + core
            part = slot(rowwise, source)
            wait_bytes(part, line_recv.at[which, n])
            send_to(part, part, bulk_send.at[2 + which], bulk_recv.at[2 + which], sibling)

    def gather_plane(which, column):
        wait_bytes(column.at[pl.ds(0, 15 * shard)], bulk_recv.at[which])

    def gather_line(which, rowwise):
        wait_bytes(rowwise.at[pl.ds(0, 8 * shard)], bulk_recv.at[2 + which])

    def send(ex, along_line):
        peers, me = (line_at, line_me) if along_line else (plane_at, plane_me)
        for peer in peers:
            send_to(msg.at[ex], got.at[ex, me], ex_send.at[ex], ex_recv.at[ex], peer)
        got[ex, me] = msg[ex]

    def receive(ex):
        wait_bytes(got.at[ex, pl.ds(0, GROUP - 1)], ex_recv.at[ex])

    def combined(ex):
        parts = got[ex]
        peak = jnp.max(parts, 0)
        return peak + log2(jnp.sum(jnp.exp2(parts - peak[None]), 0))

    def spread(index, out):
        for k in range(tiles):
            out[k * LANES : (k + 1) * LANES, :] = jnp.broadcast_to(dense[index, k : k + 1, :], (LANES, LANES)).T

    def half_norms(block_ref, out, index):
        v = block_ref[...].astype(jnp.float32)
        v = v * v
        high = v.astype(jnp.bfloat16)
        rest = (v - high.astype(jnp.float32)).astype(jnp.bfloat16)
        if out is not None:
            ones = jnp.full((v.shape[1], LANES), 1.0, jnp.bfloat16)
            out[...] = (-0.5 * LOG2E) * (
                jnp.dot(high, ones, preferred_element_type=jnp.float32)
                + jnp.dot(rest, ones, preferred_element_type=jnp.float32)
            )
        if index is not None:
            ones = jnp.full((8, v.shape[1]), 1.0, jnp.bfloat16)
            dims = (((1,), (1,)), ((), ()))
            value = (-0.5 * LOG2E) * (
                lax.dot_general(ones, high, dims, preferred_element_type=jnp.float32)
                + lax.dot_general(ones, rest, dims, preferred_element_type=jnp.float32)
            )
            for k in range(tiles):
                dense[index, k : k + 1, :] = value[0:1, k * LANES : (k + 1) * LANES]

    def products(left, right, out, norm_left=None, norm_right=None):
        wide = 2 * LANES
        for k in range(0, tiles, 2):
            both = LOG2E * lax.dot_general(
                left[...],
                right[k * LANES : k * LANES + wide, :],
                (((1,), (1,)), ((), ())),
                preferred_element_type=jnp.float32,
            )
            for h in range(2):
                part = both[:, h * LANES : (h + 1) * LANES]
                if norm_left is not None:
                    part = jnp.exp2(part + norm_left[...] + dense[norm_right, k + h : k + h + 1, :])
                out[k + h] = part

    def partial_lse(scores, potential, ex):
        part, together = 64, 3

        def step(first, carry):
            state = [None] * together
            for n in range(block // part):
                rows = pl.ds(n * part, part)
                p = potential[rows, :]
                for u in range(together):
                    s = (scores[first * together + u, rows, :] + p).reshape(part // 8, 8, LANES)
                    peak = jnp.max(s, 0)
                    total = jnp.sum(jnp.exp2(s - peak[None]), 0)
                    if n:
                        both = jnp.maximum(state[u][0], peak)
                        total = state[u][1] * jnp.exp2(state[u][0] - both) + total * jnp.exp2(peak - both)
                        peak = both
                    state[u] = (peak, total)
            for u, (peak, total) in enumerate(state):
                top = jnp.max(peak, 0, keepdims=True)
                msg[ex, pl.ds(first * together + u, 1), :] = top + log2(
                    jnp.sum(total * jnp.exp2(peak - top), 0, keepdims=True)
                )
            return carry

        lax.fori_loop(0, tiles // together, step, 0)

    def tile_sums(tile_ref, v_column, v_row, ex_row, ex_col):
        part, together = 32, 3

        def step(first, carry):
            down = list(carry)
            for u in range(together):
                n = first * together + u
                across = []
                for g in range(LANES // part):
                    rows = pl.ds(pl.multiple_of(n * LANES + g * part, part), part)
                    total = None
                    for k in range(tiles):
                        tile = tile_ref[k, rows, :]
                        if ex_row is not None:
                            down[k] = down[k] + jnp.sum((tile * v_column[rows, :]).reshape(part // 8, 8, LANES), 0)
                        if ex_col is not None:
                            term = tile * dense[v_row, k : k + 1, :]
                            total = term if total is None else total + term
                    across.append(total)
                if ex_col is not None:
                    msg[ex_col, pl.ds(n, 1), :] = jnp.sum(jnp.concatenate(across, 0).T, 0, keepdims=True)
            return tuple(down)

        first = tuple(jnp.zeros((8, LANES), jnp.float32) for _ in range(tiles if ex_row is not None else 0))
        down = lax.fori_loop(0, tiles // together, step, first)
        for k, value in enumerate(down):
            msg[ex_row, k : k + 1, :] = jnp.sum(value, 0, keepdims=True)

    def scaled_tile(scores, potential, index, ex):
        part, together = 64, 3

        def step(first, carry):
            total = [jnp.zeros((8, LANES), jnp.float32)] * together
            for n in range(block // part):
                rows = pl.ds(n * part, part)
                p = potential[rows, :]
                for u in range(together):
                    k = first * together + u
                    tile = jnp.exp2(scores[k, rows, :] + p + dense[index, pl.ds(k, 1), :])
                    scores[k, rows, :] = tile
                    total[u] = total[u] + jnp.sum(tile.reshape(part // 8, 8, LANES), 0)
            for u in range(together):
                msg[ex, pl.ds(first * together + u, 1), :] = jnp.sum(total[u], 0, keepdims=True)
            return carry

        lax.fori_loop(0, tiles // together, step, 0)

    D_F, D_G, D_NX, D_NY, D_VXR, D_VXC, D_VYR, D_VYC, D_U, D_V = range(10)

    def cross_update(ex, index, out):
        receive(ex)
        dense[index] = log_n - combined(ex)
        if out is not None:
            spread(index, out)

    def scale_update(ex, index, out):
        receive(ex)
        dense[index] = points / jnp.sum(got[ex], 0)
        if out is not None:
            spread(index, out)

    def self_update(ex, index, out):
        receive(ex)
        dense[index] = jnp.sqrt(dense[index] * points / jnp.sum(got[ex], 0))
        if out is not None:
            spread(index, out)

    def moved(index, weight, rows_ref):
        quarter = shard * XY
        ones = jnp.full((block, LANES), 1.0, jnp.bfloat16)
        for dx in (2, 1, 3, 0):
            qx = (px + dx) % XY
            rows = pl.ds(pl.multiple_of(qx * quarter, 16), quarter)
            low = jnp.concatenate([weight(k, rows).astype(jnp.bfloat16) for k in range(tiles)], 1)
            product = jnp.dot(low, rows_ref[...], preferred_element_type=jnp.float32)
            total = jnp.dot(low, ones, preferred_element_type=jnp.float32)
            for k in range(2):
                lanes = pl.ds(k * LANES, LANES)
                value = product[:, k * LANES : (k + 1) * LANES] - total * yc[rows, lanes].astype(jnp.float32)
                o_send[index, rows, lanes] = value.astype(jnp.bfloat16)
            for dy in (2, 1, 3, 0):
                if dx or dy:
                    send_to(
                        slot(o_send.at[index], qx * XY + (py + dy) % XY), o_got.at[index, plane_me],
                        bulk_send.at[4 + index], bulk_recv.at[4 + index], at(dx, dy, 0, 0),
                    )
        o_got[index, plane_me] = o_send[index, pl.ds(pl.multiple_of(plane_me * shard, 16), shard), :]

    def plan_yy(k, rows):
        return y_own[k, rows, :] * dense[D_VYR, k : k + 1, :]

    def plan_xy(k, rows):
        return a_row[k, rows, :] * dense[D_U, k : k + 1, :]

    gather(0, yc, xr)
    gather(1, None, yr)
    gather_forward(0, xr)
    gather_plane(0, yc)
    half_norms(yc, b_ny, None)
    gather_line(0, xr)
    products(yc, xr, a_row)
    partial_lse(a_row, b_ny, E_XY[0])
    send(E_XY[0], True)

    gather(1, xc, None)
    products(xr, yc, a_col)
    half_norms(xr, None, D_NX)
    gather_forward(1, yr)
    gather_line(1, yr)
    half_norms(yr, None, D_NY)
    products(yc, yr, y_own, b_ny, D_NY)
    tile_sums(y_own, b_vy, D_VYR, E_YR[0], E_YC[0])
    send(E_YR[0], True)
    send(E_YC[0], False)

    cross_update(E_XY[0], D_F, b_f)
    partial_lse(a_col, b_f, E_XY[1])
    send(E_XY[1], False)

    gather_plane(1, xc)
    half_norms(xc, b_nx, None)
    products(xc, xr, x_own, b_nx, D_NX)
    self_update(E_YR[0], D_VYR, None)
    self_update(E_YC[0], D_VYC, b_vy)
    tile_sums(y_own, b_vy, D_VYR, E_YR[1], E_YC[1])
    send(E_YR[1], True)
    send(E_YC[1], False)

    cross_update(E_XY[1], D_G, b_g)
    scaled_tile(a_row, b_g, D_F, E_XY[2])
    send(E_XY[2], True)

    tile_sums(x_own, b_vx, D_VXR, E_XR[0], E_XC[0])
    send(E_XR[0], True)
    send(E_XC[0], False)
    self_update(E_YR[1], D_VYR, None)
    self_update(E_YC[1], D_VYC, b_vy)
    tile_sums(y_own, b_vy, None, E_YR[2], None)
    send(E_YR[2], True)

    scale_update(E_XY[2], D_U, None)
    tile_sums(a_row, None, D_U, None, E_XY[3])
    send(E_XY[3], False)

    self_update(E_XR[0], D_VXR, None)
    self_update(E_XC[0], D_VXC, b_vx)
    tile_sums(x_own, b_vx, D_VXR, E_XR[1], E_XC[1])
    send(E_XR[1], True)
    send(E_XC[1], False)

    scale_update(E_XY[3], D_V, b_g)
    tile_sums(a_row, b_g, None, E_XY[4], None)
    send(E_XY[4], True)

    self_update(E_YR[2], D_VYR, None)
    moved(1, plan_yy, yr)
    self_update(E_XR[1], D_VXR, None)
    self_update(E_XC[1], D_VXC, None)
    tile_sums(x_own, None, D_VXR, None, E_XC[2])
    send(E_XC[2], False)

    scale_update(E_XY[4], D_U, None)
    tile_sums(a_row, None, D_U, None, E_XY[5])
    used = lax.broadcasted_iota(jnp.int32, (8, LANES), 0) < tiles
    here = jnp.where(used, dense[D_F] + log2(dense[D_U] / dense[D_VYR]) - dense[D_NX] - dense[D_NY], 0.0)
    msg[E_XY[5], tiles : tiles + 1, :] = jnp.sum(here, 0, keepdims=True)
    send(E_XY[5], False)
    moved(0, plan_xy, xr)
    self_update(E_XC[2], D_VXC, None)

    scale_update(E_XY[5], D_V, None)
    here = jnp.where(used, dense[D_G] + log2(dense[D_V] / dense[D_VXC]), 0.0)
    sum_msg[...] = jnp.sum(here, 0, keepdims=True)
    for peer in line_at:
        send_to(sum_msg, sum_got.at[line_me], ex_send.at[E_SUM], ex_recv.at[E_SUM], peer)
    sum_got[line_me] = sum_msg[...]
    others = jnp.sum(got[E_XY[5], :, tiles : tiles + 1, :], 0)
    spread(D_V, b_f)
    spread(D_VYR, b_vy)
    mine_xy = b_f[pl.ds(pl.multiple_of(plane_me * shard, 16), shard), :] * (1.0 / points)
    mine_yy = b_vy[pl.ds(pl.multiple_of(line_me * shard, 16), shard), :] * (1.0 / points)

    wait_bytes(o_got.at[1, pl.ds(0, GROUP - 1)], bulk_recv.at[5])
    moved_yy = jnp.sum(o_got[1].astype(jnp.float32), 0)
    wait_bytes(o_got.at[0, pl.ds(0, GROUP - 1)], bulk_recv.at[4])
    moved_xy = jnp.sum(o_got[0].astype(jnp.float32), 0)
    grad_ref[...] = (
        jnp.concatenate([mine_yy, mine_yy], 1) * moved_yy - jnp.concatenate([mine_xy, mine_xy], 1) * moved_xy
    )

    wait_bytes(sum_got.at[pl.ds(0, GROUP - 1)], ex_recv.at[E_SUM])
    total = jnp.sum(sum_got[...], 0) + others
    div_ref[...] = jnp.broadcast_to(
        jnp.sum(total, 1, keepdims=True) * (1.0 / (LOG2E * points)), div_ref.shape
    )

    for which, (column, rowwise) in enumerate(((yc, xr), (xc, yr))):
        wait_bytes(column.at[pl.ds(0, 15 * shard)], bulk_send.at[which])
        wait_bytes(rowwise.at[pl.ds(0, 15 * shard)], bulk_send.at[2 + which])
    for index in range(2):
        wait_bytes(o_got.at[index, pl.ds(0, GROUP - 1)], bulk_send.at[4 + index])
    wait_bytes(sum_got.at[pl.ds(0, GROUP - 1)], ex_send.at[E_SUM])
    for ex in range(E_SUM):
        wait_bytes(got.at[ex, pl.ds(0, GROUP - 1)], ex_send.at[ex])


def shards(x_obs, y_gen):
    shard, width = x_obs.shape
    block = shard * GROUP
    tiles = block // LANES
    f32, bf16 = jnp.float32, jnp.bfloat16
    div, grad = pl.pallas_call(
        kernel,
        out_shape=(jax.ShapeDtypeStruct((8, LANES), f32), jax.ShapeDtypeStruct((shard, width), f32)),
        in_specs=[pl.BlockSpec(memory_space=pltpu.HBM)] * 2,
        out_specs=(pl.BlockSpec(memory_space=pltpu.VMEM), pl.BlockSpec(memory_space=pltpu.VMEM)),
        scratch_shapes=[
            *[pltpu.VMEM((block, width), bf16)] * 4,
            *[pltpu.VMEM((tiles, block, LANES), f32)] * 4,
            *[pltpu.VMEM((block, LANES), f32)] * 6,
            pltpu.VMEM((10, 8, LANES), f32),
            pltpu.VMEM((N_EX, 8, LANES), f32),
            pltpu.VMEM((N_EX, GROUP, 8, LANES), f32),
            pltpu.VMEM((1, LANES), f32),
            pltpu.VMEM((GROUP, 1, LANES), f32),
            pltpu.VMEM((2, block, width), bf16),
            pltpu.VMEM((2, GROUP, shard, width), bf16),
            pltpu.SemaphoreType.DMA((4,)),
            pltpu.SemaphoreType.DMA((6,)),
            pltpu.SemaphoreType.DMA((6,)),
            pltpu.SemaphoreType.DMA((2, 7)),
            pltpu.SemaphoreType.DMA((N_EX,)),
            pltpu.SemaphoreType.DMA((N_EX,)),
        ],
        compiler_params=pltpu.CompilerParams(
            collective_id=0, has_side_effects=True, vmem_limit_bytes=48 * 1024 * 1024
        ),
    )(x_obs, y_gen)
    return div[0, 0], grad


def solution(mesh):
    placed = P(("rows", "cols"), None)
    return jax.shard_map(
        shards, mesh=mesh, in_specs=(placed, placed), out_specs=(P(), placed), check_vma=False
    )
```

```python
import math

import jax
import jax.numpy as jnp
from jax import lax
from jax.experimental import pallas as pl
from jax.experimental.pallas import tpu as pltpu
from jax.sharding import PartitionSpec as P

MESH = pl.DeviceIdType.MESH
LOG2E = math.log2(math.e)
LANES = 128
XY = 4
Z = 8
GROUP = 16

E_XY = (0, 1, 2, 3, 4, 5)
E_YR = (6, 7, 8)
E_YC = (9, 10)
E_XR = (11, 12)
E_XC = (13, 14, 15)
E_SUM = 16
N_EX = 17


def log2(value):
    return jnp.log(value) * LOG2E


def kernel(
    x_ref, y_ref, div_ref, grad_ref,
    xr, xc, yr, yc,
    a_col, a_row, y_own, x_own,
    b_f, b_g, b_ny, b_nx, b_vy, b_vx,
    dense, msg, got, sum_msg, sum_got, o_send, o_got,
    local_sem, bulk_send, bulk_recv, line_recv, ex_send, ex_recv,
):
    shard = xr.shape[0] // GROUP
    block = xr.shape[0]
    tiles = block // LANES
    points = block * GROUP
    log_n = math.log2(points)

    row, col = lax.axis_index("rows"), lax.axis_index("cols")
    px, core = col // 2, col % 2
    py, pz = row // Z, row % Z
    plane_me = px * XY + py
    line_me = pz * 2 + core

    def at(dx, dy, dz, dc):
        x, y, z, c = (px + dx) % XY, (py + dy) % XY, (pz + dz) % Z, (core + dc) % 2
        return (y * Z + z, x * 2 + c)

    plane = [
        (dx, dy, 0, 0)
        for dx, dy in (
            (2, 2), (1, 2), (3, 2), (2, 1), (2, 3), (1, 1), (3, 3), (1, 3), (3, 1),
            (2, 0), (0, 2), (1, 0), (0, 1), (3, 0), (0, 3),
        )
    ]
    hops = (4, 3, 5, 2, 6, 1, 7)
    line = [(0, 0, dz, dc) for dz in hops for dc in (1, 0)] + [(0, 0, 0, 1)]
    plane_at = [at(*p) for p in plane]
    line_at = [at(*p) for p in line]
    line_same = [at(0, 0, dz, 0) for dz in hops]
    sibling = at(0, 0, 0, 1)

    def slot(ref, index):
        return ref.at[pl.ds(pl.multiple_of(index * shard, 16), shard)]

    barrier = pltpu.get_barrier_semaphore()
    for peer in line_at + plane_at:
        pl.semaphore_signal(barrier, inc=1, device_id=peer, device_id_type=MESH)

    own = []
    for n, (src, ref, index) in enumerate(
        ((y_ref, yc, plane_me), (x_ref, xr, line_me), (x_ref, xc, plane_me), (y_ref, yr, line_me))
    ):
        copy = pltpu.make_async_copy(src, slot(ref, index), local_sem.at[n])
        copy.start()
        own.append(copy)
    msg[...] = jnp.ones_like(msg)
    dense[...] = jnp.ones_like(dense)
    b_vy[...] = jnp.ones_like(b_vy)
    b_vx[...] = jnp.ones_like(b_vx)
    for copy in own:
        copy.wait()
    pl.semaphore_wait(barrier, len(plane_at) + len(line_at))

    def send_to(src, dst, send, recv, peer):
        copy = pltpu.make_async_remote_copy(
            src_ref=src, dst_ref=dst, send_sem=send, recv_sem=recv, device_id=peer, device_id_type=MESH
        )
        copy.start()
        return copy

    def wait_bytes(ref, sem):
        pltpu.make_async_copy(ref, ref, sem).wait()

    def send_plane(which, column, n):
        send_to(slot(column, plane_me), slot(column, plane_me), bulk_send.at[which], bulk_recv.at[which], plane_at[n])

    def send_line(which, rowwise, n):
        part = slot(rowwise, line_me)
        if n < len(hops):
            send_to(part, part, bulk_send.at[2 + which], line_recv.at[which, n], line_same[n])
        else:
            send_to(part, part, bulk_send.at[2 + which], bulk_recv.at[2 + which], sibling)

    def gather(which, column, rowwise):
        for n in range(len(plane_at)):
            if rowwise is not None and n <= len(hops):
                send_line(which, rowwise, n)
            if column is not None:
                send_plane(which, column, n)

    def gather_forward(which, rowwise):
        for n in sorted(range(len(hops)), key=lambda n: min(hops[n], Z - hops[n])):
            source = ((pz + Z - hops[n]) % Z) * 2 + core
            part = slot(rowwise, source)
            wait_bytes(part, line_recv.at[which, n])
            send_to(part, part, bulk_send.at[2 + which], bulk_recv.at[2 + which], sibling)

    def gather_plane(which, column):
        wait_bytes(column.at[pl.ds(0, 15 * shard)], bulk_recv.at[which])

    def gather_line(which, rowwise):
        wait_bytes(rowwise.at[pl.ds(0, 8 * shard)], bulk_recv.at[2 + which])

    def send(ex, along_line):
        peers, me = (line_at, line_me) if along_line else (plane_at, plane_me)
        for peer in peers:
            send_to(msg.at[ex], got.at[ex, me], ex_send.at[ex], ex_recv.at[ex], peer)
        got[ex, me] = msg[ex]

    def receive(ex):
        wait_bytes(got.at[ex, pl.ds(0, GROUP - 1)], ex_recv.at[ex])

    def combined(ex):
        parts = got[ex]
        peak = jnp.max(parts, 0)
        return peak + log2(jnp.sum(jnp.exp2(parts - peak[None]), 0))

    def spread(index, out):
        for k in range(tiles):
            out[k * LANES : (k + 1) * LANES, :] = jnp.broadcast_to(dense[index, k : k + 1, :], (LANES, LANES)).T

    def half_norms(block_ref, out, index):
        v = block_ref[...].astype(jnp.float32)
        v = v * v
        high = v.astype(jnp.bfloat16)
        rest = (v - high.astype(jnp.float32)).astype(jnp.bfloat16)
        if out is not None:
            ones = jnp.full((v.shape[1], LANES), 1.0, jnp.bfloat16)
            out[...] = (-0.5 * LOG2E) * (
                jnp.dot(high, ones, preferred_element_type=jnp.float32)
                + jnp.dot(rest, ones, preferred_element_type=jnp.float32)
            )
        if index is not None:
            ones = jnp.full((8, v.shape[1]), 1.0, jnp.bfloat16)
            dims = (((1,), (1,)), ((), ()))
            value = (-0.5 * LOG2E) * (
                lax.dot_general(ones, high, dims, preferred_element_type=jnp.float32)
                + lax.dot_general(ones, rest, dims, preferred_element_type=jnp.float32)
            )
            for k in range(tiles):
                dense[index, k : k + 1, :] = value[0:1, k * LANES : (k + 1) * LANES]

    def products(left, right, out, norm_left=None, norm_right=None, pairs=range(0, tiles, 2)):
        wide = 2 * LANES
        for k in pairs:
            both = LOG2E * lax.dot_general(
                left[...],
                right[k * LANES : k * LANES + wide, :],
                (((1,), (1,)), ((), ())),
                preferred_element_type=jnp.float32,
            )
            for h in range(2):
                part = both[:, h * LANES : (h + 1) * LANES]
                if norm_left is not None:
                    part = jnp.exp2(part + norm_left[...] + dense[norm_right, k + h : k + h + 1, :])
                out[k + h] = part

    def reduce_tiles(scores, potential, ex, which):
        part = 64
        state = [None] * len(which)
        for n in range(block // part):
            rows = pl.ds(n * part, part)
            p = potential[rows, :]
            for u, k in enumerate(which):
                s = (scores[k, rows, :] + p).reshape(part // 8, 8, LANES)
                peak = jnp.max(s, 0)
                total = jnp.sum(jnp.exp2(s - peak[None]), 0)
                if n:
                    both = jnp.maximum(state[u][0], peak)
                    total = state[u][1] * jnp.exp2(state[u][0] - both) + total * jnp.exp2(peak - both)
                    peak = both
                state[u] = (peak, total)
        for (peak, total), k in zip(state, which):
            top = jnp.max(peak, 0, keepdims=True)
            msg[ex, k : k + 1, :] = top + log2(jnp.sum(total * jnp.exp2(peak - top), 0, keepdims=True))

    def partial_lse(scores, potential, ex):
        part, together = 64, 3

        def step(first, carry):
            state = [None] * together
            for n in range(block // part):
                rows = pl.ds(n * part, part)
                p = potential[rows, :]
                for u in range(together):
                    s = (scores[first * together + u, rows, :] + p).reshape(part // 8, 8, LANES)
                    peak = jnp.max(s, 0)
                    total = jnp.sum(jnp.exp2(s - peak[None]), 0)
                    if n:
                        both = jnp.maximum(state[u][0], peak)
                        total = state[u][1] * jnp.exp2(state[u][0] - both) + total * jnp.exp2(peak - both)
                        peak = both
                    state[u] = (peak, total)
            for u, (peak, total) in enumerate(state):
                top = jnp.max(peak, 0, keepdims=True)
                msg[ex, pl.ds(first * together + u, 1), :] = top + log2(
                    jnp.sum(total * jnp.exp2(peak - top), 0, keepdims=True)
                )
            return carry

        lax.fori_loop(0, tiles // together, step, 0)

    def tile_sums(tile_ref, v_column, v_row, ex_row, ex_col):
        part, together = 32, 3

        def step(first, carry):
            down = list(carry)
            for u in range(together):
                n = first * together + u
                across = []
                for g in range(LANES // part):
                    rows = pl.ds(pl.multiple_of(n * LANES + g * part, part), part)
                    total = None
                    for k in range(tiles):
                        tile = tile_ref[k, rows, :]
                        if ex_row is not None:
                            down[k] = down[k] + jnp.sum((tile * v_column[rows, :]).reshape(part // 8, 8, LANES), 0)
                        if ex_col is not None:
                            term = tile * dense[v_row, k : k + 1, :]
                            total = term if total is None else total + term
                    across.append(total)
                if ex_col is not None:
                    msg[ex_col, pl.ds(n, 1), :] = jnp.sum(jnp.concatenate(across, 0).T, 0, keepdims=True)
            return tuple(down)

        first = tuple(jnp.zeros((8, LANES), jnp.float32) for _ in range(tiles if ex_row is not None else 0))
        down = lax.fori_loop(0, tiles // together, step, first)
        for k, value in enumerate(down):
            msg[ex_row, k : k + 1, :] = jnp.sum(value, 0, keepdims=True)

    def scaled_tile(scores, potential, index, ex):
        part, together = 64, 3

        def step(first, carry):
            total = [jnp.zeros((8, LANES), jnp.float32)] * together
            for n in range(block // part):
                rows = pl.ds(n * part, part)
                p = potential[rows, :]
                for u in range(together):
                    k = first * together + u
                    tile = jnp.exp2(scores[k, rows, :] + p + dense[index, pl.ds(k, 1), :])
                    scores[k, rows, :] = tile
                    total[u] = total[u] + jnp.sum(tile.reshape(part // 8, 8, LANES), 0)
            for u in range(together):
                msg[ex, pl.ds(first * together + u, 1), :] = jnp.sum(total[u], 0, keepdims=True)
            return carry

        lax.fori_loop(0, tiles // together, step, 0)

    D_F, D_G, D_NX, D_NY, D_VXR, D_VXC, D_VYR, D_VYC, D_U, D_V = range(10)

    def cross_update(ex, index, out):
        receive(ex)
        dense[index] = log_n - combined(ex)
        if out is not None:
            spread(index, out)

    def scale_update(ex, index, out):
        receive(ex)
        dense[index] = points / jnp.sum(got[ex], 0)
        if out is not None:
            spread(index, out)

    def self_update(ex, index, out):
        receive(ex)
        dense[index] = jnp.sqrt(dense[index] * points / jnp.sum(got[ex], 0))
        if out is not None:
            spread(index, out)

    def moved(index, weight, rows_ref):
        quarter = shard * XY
        ones = jnp.full((block, LANES), 1.0, jnp.bfloat16)
        for dx in (2, 1, 3, 0):
            qx = (px + dx) % XY
            rows = pl.ds(pl.multiple_of(qx * quarter, 16), quarter)
            low = jnp.concatenate([weight(k, rows).astype(jnp.bfloat16) for k in range(tiles)], 1)
            product = jnp.dot(low, rows_ref[...], preferred_element_type=jnp.float32)
            total = jnp.dot(low, ones, preferred_element_type=jnp.float32)
            for k in range(2):
                lanes = pl.ds(k * LANES, LANES)
                value = product[:, k * LANES : (k + 1) * LANES] - total * yc[rows, lanes].astype(jnp.float32)
                o_send[index, rows, lanes] = value.astype(jnp.bfloat16)
            for dy in (2, 1, 3, 0):
                if dx or dy:
                    send_to(
                        slot(o_send.at[index], qx * XY + (py + dy) % XY), o_got.at[index, plane_me],
                        bulk_send.at[4 + index], bulk_recv.at[4 + index], at(dx, dy, 0, 0),
                    )
        o_got[index, plane_me] = o_send[index, pl.ds(pl.multiple_of(plane_me * shard, 16), shard), :]

    def plan_yy(k, rows):
        return y_own[k, rows, :] * dense[D_VYR, k : k + 1, :]

    def plan_xy(k, rows):
        return a_row[k, rows, :] * dense[D_U, k : k + 1, :]

    gather(0, yc, xr)
    gather(1, None, yr)
    gather_forward(0, xr)
    gather_plane(0, yc)
    half_norms(yc, b_ny, None)
    gather_line(0, xr)
    for first in range(0, tiles, 2):
        products(yc, xr, a_row, pairs=(first,))
        reduce_tiles(a_row, b_ny, E_XY[0], (first, first + 1))
    send(E_XY[0], True)

    gather(1, xc, None)
    products(xr, yc, a_col)
    half_norms(xr, None, D_NX)
    gather_forward(1, yr)
    gather_line(1, yr)
    half_norms(yr, None, D_NY)
    products(yc, yr, y_own, b_ny, D_NY)
    tile_sums(y_own, b_vy, D_VYR, E_YR[0], E_YC[0])
    send(E_YR[0], True)
    send(E_YC[0], False)

    cross_update(E_XY[0], D_F, b_f)
    partial_lse(a_col, b_f, E_XY[1])
    send(E_XY[1], False)

    gather_plane(1, xc)
    half_norms(xc, b_nx, None)
    products(xc, xr, x_own, b_nx, D_NX)
    self_update(E_YR[0], D_VYR, None)
    self_update(E_YC[0], D_VYC, b_vy)
    tile_sums(y_own, b_vy, D_VYR, E_YR[1], E_YC[1])
    send(E_YR[1], True)
    send(E_YC[1], False)

    cross_update(E_XY[1], D_G, b_g)
    scaled_tile(a_row, b_g, D_F, E_XY[2])
    send(E_XY[2], True)

    tile_sums(x_own, b_vx, D_VXR, E_XR[0], E_XC[0])
    send(E_XR[0], True)
    send(E_XC[0], False)
    self_update(E_YR[1], D_VYR, None)
    self_update(E_YC[1], D_VYC, b_vy)
    tile_sums(y_own, b_vy, None, E_YR[2], None)
    send(E_YR[2], True)

    scale_update(E_XY[2], D_U, None)
    tile_sums(a_row, None, D_U, None, E_XY[3])
    send(E_XY[3], False)

    self_update(E_XR[0], D_VXR, None)
    self_update(E_XC[0], D_VXC, b_vx)
    tile_sums(x_own, b_vx, D_VXR, E_XR[1], E_XC[1])
    send(E_XR[1], True)
    send(E_XC[1], False)

    scale_update(E_XY[3], D_V, b_g)
    tile_sums(a_row, b_g, None, E_XY[4], None)
    send(E_XY[4], True)

    self_update(E_YR[2], D_VYR, None)
    moved(1, plan_yy, yr)
    self_update(E_XR[1], D_VXR, None)
    self_update(E_XC[1], D_VXC, None)
    tile_sums(x_own, None, D_VXR, None, E_XC[2])
    send(E_XC[2], False)

    scale_update(E_XY[4], D_U, None)
    tile_sums(a_row, None, D_U, None, E_XY[5])
    used = lax.broadcasted_iota(jnp.int32, (8, LANES), 0) < tiles
    here = jnp.where(used, dense[D_F] + log2(dense[D_U] / dense[D_VYR]) - dense[D_NX] - dense[D_NY], 0.0)
    msg[E_XY[5], tiles : tiles + 1, :] = jnp.sum(here, 0, keepdims=True)
    send(E_XY[5], False)
    moved(0, plan_xy, xr)
    self_update(E_XC[2], D_VXC, None)

    scale_update(E_XY[5], D_V, None)
    here = jnp.where(used, dense[D_G] + log2(dense[D_V] / dense[D_VXC]), 0.0)
    sum_msg[...] = jnp.sum(here, 0, keepdims=True)
    for peer in line_at:
        send_to(sum_msg, sum_got.at[line_me], ex_send.at[E_SUM], ex_recv.at[E_SUM], peer)
    sum_got[line_me] = sum_msg[...]
    others = jnp.sum(got[E_XY[5], :, tiles : tiles + 1, :], 0)
    spread(D_V, b_f)
    spread(D_VYR, b_vy)
    mine_xy = b_f[pl.ds(pl.multiple_of(plane_me * shard, 16), shard), :] * (1.0 / points)
    mine_yy = b_vy[pl.ds(pl.multiple_of(line_me * shard, 16), shard), :] * (1.0 / points)

    wait_bytes(o_got.at[1, pl.ds(0, GROUP - 1)], bulk_recv.at[5])
    moved_yy = jnp.sum(o_got[1].astype(jnp.float32), 0)
    wait_bytes(o_got.at[0, pl.ds(0, GROUP - 1)], bulk_recv.at[4])
    moved_xy = jnp.sum(o_got[0].astype(jnp.float32), 0)
    grad_ref[...] = (
        jnp.concatenate([mine_yy, mine_yy], 1) * moved_yy - jnp.concatenate([mine_xy, mine_xy], 1) * moved_xy
    )

    wait_bytes(sum_got.at[pl.ds(0, GROUP - 1)], ex_recv.at[E_SUM])
    total = jnp.sum(sum_got[...], 0) + others
    div_ref[...] = jnp.broadcast_to(
        jnp.sum(total, 1, keepdims=True) * (1.0 / (LOG2E * points)), div_ref.shape
    )

    for which, (column, rowwise) in enumerate(((yc, xr), (xc, yr))):
        wait_bytes(column.at[pl.ds(0, 15 * shard)], bulk_send.at[which])
        wait_bytes(rowwise.at[pl.ds(0, 15 * shard)], bulk_send.at[2 + which])
    for index in range(2):
        wait_bytes(o_got.at[index, pl.ds(0, GROUP - 1)], bulk_send.at[4 + index])
    wait_bytes(sum_got.at[pl.ds(0, GROUP - 1)], ex_send.at[E_SUM])
    for ex in range(E_SUM):
        wait_bytes(got.at[ex, pl.ds(0, GROUP - 1)], ex_send.at[ex])


def shards(x_obs, y_gen):
    shard, width = x_obs.shape
    block = shard * GROUP
    tiles = block // LANES
    f32, bf16 = jnp.float32, jnp.bfloat16
    div, grad = pl.pallas_call(
        kernel,
        out_shape=(jax.ShapeDtypeStruct((8, LANES), f32), jax.ShapeDtypeStruct((shard, width), f32)),
        in_specs=[pl.BlockSpec(memory_space=pltpu.HBM)] * 2,
        out_specs=(pl.BlockSpec(memory_space=pltpu.VMEM), pl.BlockSpec(memory_space=pltpu.VMEM)),
        scratch_shapes=[
            *[pltpu.VMEM((block, width), bf16)] * 4,
            *[pltpu.VMEM((tiles, block, LANES), f32)] * 4,
            *[pltpu.VMEM((block, LANES), f32)] * 6,
            pltpu.VMEM((10, 8, LANES), f32),
            pltpu.VMEM((N_EX, 8, LANES), f32),
            pltpu.VMEM((N_EX, GROUP, 8, LANES), f32),
            pltpu.VMEM((1, LANES), f32),
            pltpu.VMEM((GROUP, 1, LANES), f32),
            pltpu.VMEM((2, block, width), bf16),
            pltpu.VMEM((2, GROUP, shard, width), bf16),
            pltpu.SemaphoreType.DMA((4,)),
            pltpu.SemaphoreType.DMA((6,)),
            pltpu.SemaphoreType.DMA((6,)),
            pltpu.SemaphoreType.DMA((2, 7)),
            pltpu.SemaphoreType.DMA((N_EX,)),
            pltpu.SemaphoreType.DMA((N_EX,)),
        ],
        compiler_params=pltpu.CompilerParams(
            collective_id=0, has_side_effects=True, vmem_limit_bytes=48 * 1024 * 1024
        ),
    )(x_obs, y_gen)
    return div[0, 0], grad


def solution(mesh):
    placed = P(("rows", "cols"), None)
    return jax.shard_map(
        shards, mesh=mesh, in_specs=(placed, placed), out_specs=(P(), placed), check_vma=False
    )
```
